32 devices in a mesh: wide: 16 (over z, y, x), narrow: 2 (over core).
Axes of the slice: x: 2, y: 2, z: 4, core: 2. Of those that a mesh axis runs over, the one named last changes fastest.
Arguments:
- tokens_in: bfloat16 [256, 128, 256], P('wide'), may hold values from -8 to 8
- visible: int32 [256, 128], P('wide'), may hold values 0 or 1
- traj_start: int32 [256], P('wide'), may hold values from 0 to 936
- cotangent: bfloat16 [256, 128, 256], P('wide'), may hold values from -6 to 6
- mask_token: bfloat16 [256], replicated, may hold values from -6 to 6
- time_table: bfloat16 [1000, 256], replicated, may hold values from -3 to 3
- gain_one: float32 [256], replicated, may hold values from 0.5 to 1.5
- bias_one: float32 [256], replicated, may hold values from -1.8 to 1.8
- w_qkv: bfloat16 [256, 3, 256], P(None, None, 'narrow'), may hold values from -0.375 to 0.375
- query_bias: bfloat16 [256], P('narrow'), may hold values from -3 to 3
- value_bias: bfloat16 [256], P('narrow'), may hold values from -3 to 3
- w_out: bfloat16 [256, 256], P('narrow'), may hold values from -1.5 to 1.5
- out_bias: bfloat16 [256], replicated, may hold values from -3 to 3
- gain_two: float32 [256], replicated, may hold values from 0.5 to 1.5
- bias_two: float32 [256], replicated, may hold values from -1.8 to 1.8
- w_up: bfloat16 [256, 1024], P(None, 'narrow'), may hold values from -0.375 to 0.375
- up_bias: bfloat16 [1024], P('narrow'), may hold values from -3 to 3
- w_down: bfloat16 [1024, 256], P('narrow'), may hold values from -0.1875 to 0.1875
- down_bias: bfloat16 [256], replicated, may hold values from -3 to 3
Outputs:
- output: bfloat16 [256, 128, 256], P('wide')
- input_grad: bfloat16 [256, 128, 256], P('wide')
- grad_mask_token: float32 [256], replicated
- grad_time: float32 [1000, 256], replicated
- grad_gain_one: float32 [256], replicated
- grad_bias_one: float32 [256], replicated
- grad_qkv: float32 [256, 3, 256], P(None, None, 'narrow')
- grad_query_bias: float32 [256], P('narrow')
- grad_value_bias: float32 [256], P('narrow')
- grad_out_w: float32 [256, 256], P('narrow')
- grad_out_bias: float32 [256], replicated
- grad_gain_two: float32 [256], replicated
- grad_bias_two: float32 [256], replicated
- grad_up: float32 [256, 1024], P(None, 'narrow')
- grad_up_bias: float32 [1024], P('narrow')
- grad_down: float32 [1024, 256], P('narrow')
- grad_down_bias: float32 [256], replicated
- rms_stats: float32 [3], replicated
The draws below stay inside these ranges and needn't reach their ends.
All inputs are finite; a program needn't handle non-finite values. No bound on the sum of `visible` on one device may be relied on, other than what follows from the above.
Results may differ from the reference program's by a relative error of at most 0.018.
Values may be sent and summed in bfloat16 or wider, within the bound.
No kernel may reach another device: no remote copies, remote signals or barrier semaphores. Data moves between devices by JAX's collectives and lax.ppermute only.
A program may use at most 128 MiB of HBM per device.

```python
import math
import jax
import jax.numpy as jnp
from jax import lax

D = 256
HEADS = 4
HEAD_DIM = 64
FF = 1024
TMAX = 1000
L = 128
TRAJ = 256


def draw_tokens_in(key, part):
    key = jax.random.fold_in(key, 11)
    ramp = 0.6 + 1.2 * jnp.arange(TRAJ, dtype=jnp.float32) / TRAJ
    values_drawn = jax.random.normal(key, (TRAJ, L, D), jnp.float32) * ramp[:, None, None]
    return jnp.clip(values_drawn, -8.0, 8.0).astype(jnp.bfloat16)


def with_ends(drawn, stream_key, smallest, high):
    extent = drawn.shape
    place = [jax.random.randint(jax.random.fold_in(stream_key, axis), (), 0, extent[axis]) for axis in range(len(extent))]
    drawn = drawn.at[tuple(place)].set(smallest)
    longest = extent.index(max(extent))
    place[longest] = (place[longest] + 1) % extent[longest]
    return drawn.at[tuple(place)].set(high)


def block_levels(own_key, shape, cuts, low, top_value):
    def one(axis_at, shards_of):
        draws = jax.random.uniform(jax.random.fold_in(jax.random.fold_in(own_key, 6), axis_at), (shards_of,), jnp.float32, low / len(cuts), top_value / len(cuts))
        return jnp.repeat(jnp.exp(draws), shape[axis_at] // shards_of).reshape((-1,) + (1,) * (len(shape) - axis_at - 1))

    factor_of = one(*cuts[0])
    for cut in cuts[1:]:
        factor_of = factor_of * one(*cut)
    return factor_of


def bell_draw(stream_key, extent, scale, most, cuts=(), kind=jnp.bfloat16):
    factor_of = block_levels(stream_key, extent, cuts, -0.22, 0.18) if cuts else 1.0
    values = jax.random.normal(stream_key, extent, jnp.float32) * scale * factor_of
    return jnp.minimum(jnp.maximum(values, -most), most).astype(kind)


def setup_inputs(seed: int = 0) -> dict:
    streams_of = jax.random.split(jax.random.key(seed), 20)
    tokens_in = draw_tokens_in(jax.random.fold_in(streams_of[19], 71), 0)
    visible = with_ends((jax.random.randint(streams_of[1], (TRAJ, L), 0, 2) < 1).astype(jnp.int32), jax.random.fold_in(streams_of[1], 1), 0, 1)
    traj_start = with_ends(jax.random.randint(streams_of[2], (TRAJ,), 0, TMAX - L // 2 + 1), jax.random.fold_in(streams_of[2], 1), 0, (TMAX - L // 2 + 1) - 1).astype(jnp.int32)
    cotangent = bell_draw(streams_of[3], (TRAJ, L, D), 1.0, 6.0, ((0, 16),))
    mask_token = bell_draw(streams_of[4], (D,), 1.0, 6.0)
    time_table = bell_draw(streams_of[5], (TMAX, D), 0.5, 3.0)
    gain_one = jnp.clip(1.0 + 0.1 * jax.random.normal(streams_of[6], (D,), jnp.float32), 0.5, 1.5)
    bias_one = bell_draw(streams_of[7], (D,), 0.3, 1.8, (), jnp.float32)
    w_qkv = bell_draw(streams_of[8], (D, 3, D), D ** -0.5, 0.375, ((2, 2),))
    query_bias = bell_draw(streams_of[9], (D,), 0.5, 3.0, ((0, 2),))
    value_bias = bell_draw(streams_of[10], (D,), 0.5, 3.0, ((0, 2),))
    w_out = bell_draw(streams_of[11], (D, D), (D // 16) ** -0.5, 1.5, ((0, 2),))
    out_bias = bell_draw(streams_of[12], (D,), 0.5, 3.0)
    gain_two = jnp.clip(1.0 + 0.1 * jax.random.normal(streams_of[13], (D,), jnp.float32), 0.5, 1.5)
    bias_two = bell_draw(streams_of[14], (D,), 0.3, 1.8, (), jnp.float32)
    w_up = bell_draw(streams_of[15], (D, FF), D ** -0.5, 0.375, ((1, 2),))
    up_bias = bell_draw(streams_of[16], (FF,), 0.5, 3.0, ((0, 2),))
    w_down = bell_draw(streams_of[17], (FF, D), FF ** -0.5, 0.1875, ((0, 2),))
    down_bias = bell_draw(streams_of[18], (D,), 0.5, 3.0)
    return dict(tokens_in=tokens_in, visible=visible, traj_start=traj_start, cotangent=cotangent, mask_token=mask_token, time_table=time_table, gain_one=gain_one, bias_one=bias_one, w_qkv=w_qkv, query_bias=query_bias, value_bias=value_bias, w_out=w_out, out_bias=out_bias, gain_two=gain_two, bias_two=bias_two, w_up=w_up, up_bias=up_bias, w_down=w_down, down_bias=down_bias)


@jax.custom_vjp
def low(v):
    return lax.optimization_barrier(v.astype(jnp.bfloat16)).astype(jnp.float32)

@jax.custom_vjp
def low_back(v):
    return v

def low_keep(v):
    return (low(v), None)

def low_pass(kept, grad):
    return (grad,)

def back_keep(v):
    return (v, None)

def back_low(kept, grad):
    return (low(grad),)
low.defvjp(low_keep, low_pass)
low_back.defvjp(back_keep, back_low)
epsilon = 1e-05
highest = lax.Precision.HIGHEST

def layer_norm(stream, norm_gain, norm_shift):
    centre = stream - lax.optimization_barrier(jnp.mean(stream, axis=-1, keepdims=True))
    spread = lax.optimization_barrier(jnp.mean(centre * centre, axis=-1, keepdims=True))
    return centre * lax.rsqrt(spread + epsilon) * norm_gain + norm_shift

def block_forward(weights, tokens_in, visible, traj_start):
    mask_token, time_table, gain_one, bias_one, w_qkv, query_bias, value_bias, w_out, out_bias, gain_two, bias_two, w_up, up_bias, w_down, down_bias = weights
    traj_count = tokens_in.shape[0]
    half_steps = jnp.arange(L, dtype=jnp.int32) // 2
    step_index = (traj_start[:, None] + half_steps[None, :]).astype(jnp.int32)
    embedded = jnp.take(time_table, step_index, axis=0)
    stream = jnp.where(visible[:, :, None] == 1, tokens_in, mask_token) + embedded
    normed_one = low(layer_norm(stream, gain_one, bias_one))
    bias_rows = jnp.stack([query_bias, jnp.zeros_like(query_bias), value_bias])
    project = jnp.einsum('gsd,dce->gsce', normed_one, w_qkv, precision=highest) + bias_rows
    project = low(low_back(project)).reshape(traj_count, L, 3, HEADS, HEAD_DIM)
    queries = project[:, :, 0]
    keys_all = project[:, :, 1]
    values_all = project[:, :, 2]
    score_scale = 1.0 / math.sqrt(HEAD_DIM)
    scores = low_back(jnp.einsum('gqhe,gkhe->ghqk', queries, keys_all, precision=highest) * score_scale)
    attn_probs = low(jax.nn.softmax(scores, axis=-1))
    context = jnp.einsum('ghqk,gkhe->gqhe', attn_probs, values_all, precision=highest).reshape(traj_count, L, D)
    context = low(low_back(context))
    branch_attn = low_back(jnp.einsum('gse,ed->gsd', context, w_out, precision=highest) + out_bias)
    hidden_stream = stream + branch_attn
    normed_two = low(layer_norm(hidden_stream, gain_two, bias_two))
    pre_act = low_back(jnp.einsum('gsd,df->gsf', normed_two, w_up, precision=highest) + up_bias)
    activated = low(jax.nn.gelu(pre_act))
    branch_mlp = low_back(jnp.einsum('gsf,fd->gsd', activated, w_down, precision=highest) + down_bias)
    result = hidden_stream + branch_mlp
    square_sums = jnp.stack([jnp.sum(stream * stream), jnp.sum(branch_attn * branch_attn), jnp.sum(branch_mlp * branch_mlp)])
    return (result, square_sums)

def reference(tokens_in, visible, traj_start, cotangent, mask_token, time_table, gain_one, bias_one, w_qkv, query_bias, value_bias, w_out, out_bias, gain_two, bias_two, w_up, up_bias, w_down, down_bias):
    weights = jax.tree.map(lambda element: element.astype(jnp.float32), (mask_token, time_table, gain_one, bias_one, w_qkv, query_bias, value_bias, w_out, out_bias, gain_two, bias_two, w_up, up_bias, w_down, down_bias))
    group_size = 32
    group_count = TRAJ // group_size

    def shape_groups(array):
        return array.reshape((group_count, group_size) + array.shape[1:])

    def one_group(running, pieces):
        grad_running, stat_running = running
        tokens_grp, visible_grp, start_grp, cotan_grp = pieces

        def forward_fn(weights_in, tokens_float):
            return block_forward(weights_in, tokens_float, visible_grp, start_grp)
        result, pullback, square_sums = jax.vjp(forward_fn, weights, tokens_grp.astype(jnp.float32), has_aux=True)
        grad_weights, grad_tokens = pullback(cotan_grp.astype(jnp.float32))
        grad_running = jax.tree.map(lambda left, right: left + right, grad_running, grad_weights)
        return ((grad_running, stat_running + square_sums), (result.astype(jnp.bfloat16), grad_tokens.astype(jnp.bfloat16)))
    start_state = (jax.tree.map(jnp.zeros_like, weights), jnp.zeros((3,), jnp.float32))
    (grad_all, stat_all), (output, input_grad) = lax.scan(one_group, start_state, (shape_groups(tokens_in), shape_groups(visible), shape_groups(traj_start), shape_groups(cotangent)))
    output = output.reshape(TRAJ, L, D)
    input_grad = input_grad.reshape(TRAJ, L, D)
    rms_stats = jnp.sqrt(stat_all / (TRAJ * L * D))
    grad_mask_token, grad_time, grad_gain_one, grad_bias_one, grad_qkv, grad_query_bias, grad_value_bias, grad_out_w, grad_out_bias, grad_gain_two, grad_bias_two, grad_up, grad_up_bias, grad_down, grad_down_bias = grad_all
    return (output, input_grad, grad_mask_token, grad_time, grad_gain_one, grad_bias_one, grad_qkv, grad_query_bias, grad_value_bias, grad_out_w, grad_out_bias, grad_gain_two, grad_bias_two, grad_up, grad_up_bias, grad_down, grad_down_bias, rms_stats)
```

```python
import functools
import math

import jax
import jax.numpy as jnp
from jax import lax
from jax.experimental import pallas as pl
from jax.experimental.pallas import tpu as pltpu
from jax.sharding import PartitionSpec as P

HEAD_DIM = 64
EPS = 1e-05
F32 = jnp.float32
BF16 = jnp.bfloat16
VMEM_LIMIT = 24 * 1024 * 1024
FIRST_ROWS = 2304
SECOND_ROWS = 1792
TIME_AT = 768
SMALL_AT = 1776
WINDOW = 128
CURVE = math.sqrt(2.0 / math.pi)


def nn(a, b):
    return lax.dot_general(a, b, (((1,), (0,)), ((), ())), preferred_element_type=F32)


def nt(a, b):
    return lax.dot_general(a, b, (((1,), (1,)), ((), ())), preferred_element_type=F32)


def tn(a, b):
    return lax.dot_general(a, b, (((0,), (0,)), ((), ())), preferred_element_type=F32)


def as_row(ref):
    return ref[...].astype(F32).reshape(1, ref.shape[0])


def row_mean(v):
    return jnp.mean(v, axis=-1, keepdims=True)


def fold_rows(v):
    return jnp.sum(v.reshape(v.shape[0] // 8, 8, v.shape[1]), axis=0)


def head_masks(scale):
    lane = lax.broadcasted_iota(jnp.int32, (1, 128), 1)
    low = jnp.where(lane < HEAD_DIM, scale, 0.0).astype(BF16)
    high = jnp.where(lane < HEAD_DIM, 0.0, scale).astype(BF16)
    return low, high


def masked_pair(v, masks):
    return jnp.concatenate([v * masks[0], v * masks[1]], axis=0)


def side_to_stack(v):
    return jnp.concatenate([v[:, :128], v[:, 128:]], axis=0)


def by_blocks(function, size, *arrays):
    parts = [
        function(*[v[k : k + size] for v in arrays]) for k in range(0, arrays[0].shape[0], size)
    ]
    return [jnp.concatenate(column, axis=0) for column in zip(*parts)]


def gelu_and_slope(shift, product, grad_act):
    pre = product + shift
    square = pre * pre
    half = 0.5 * jnp.tanh(pre * (CURVE + (CURVE * 0.044715) * square)) + 0.5
    act = pre * half
    slope = half + act * (1.0 - half) * (2.0 * CURVE + (6.0 * CURVE * 0.044715) * square)
    grad_pre = slope * grad_act
    return act.astype(BF16), grad_pre.astype(BF16), fold_rows(grad_pre)


def visible_tile(vis_ref, which):
    row = vis_ref[pl.ds(which, 1), :].astype(F32)
    tall = jnp.transpose(jnp.broadcast_to(row, (128, 128)))
    return jnp.concatenate([tall, tall], axis=1) > 0.5


def window_of(first_step, table_rows):
    begin = jnp.minimum((first_step // 8) * 8, table_rows - WINDOW)
    return pl.multiple_of(begin, 8), first_step - begin


def rows_of(index, count):
    return pl.ds(pl.multiple_of(index * count, count), count)


def pack(flip_base, acc, own_ref, oth_ref):
    size = own_ref.shape[0] // 4
    for j in range(4):
        source = rows_of(jnp.bitwise_xor(flip_base, j), size)
        for side, ref in enumerate((own_ref, oth_ref)):
            ref[j * size : j * size + size, :] = acc[side, source, :].astype(BF16)


def embed_kernel(
    mine, meta, starts_hbm, tok_hbm, vis_hbm, cot_hbm, table_hbm,
    mask_hbm, gain_one_hbm, bias_one_hbm, out_bias_hbm, gain_two_hbm, bias_two_hbm, down_bias_hbm,
    wqkv_hbm, wout_hbm, wup_hbm, wdown_hbm, query_hbm, value_hbm, up_hbm,
    stream_ref, normed_ref, cot_ref, vec_ref, bias_ref, vis_ref, wqkv_ref, wout_ref, wup_ref, wdown_ref,
    starts, tok, table, table_f32, mask, gain_one, bias_one, out_bias, gain_two, bias_two, down_bias,
    query, value, up, copied,
):
    narrow = meta[0]
    here = pl.ds(narrow * mine, mine)
    first = [
        (starts_hbm, starts), (vis_hbm, vis_ref), (table_hbm, table), (tok_hbm.at[here], tok),
        (mask_hbm, mask), (gain_one_hbm, gain_one), (bias_one_hbm, bias_one),
        (out_bias_hbm, out_bias), (gain_two_hbm, gain_two), (bias_two_hbm, bias_two),
        (down_bias_hbm, down_bias), (query_hbm, query), (value_hbm, value), (up_hbm, up),
    ]
    later = [
        (cot_hbm.at[here], cot_ref), (wqkv_hbm, wqkv_ref), (wout_hbm, wout_ref), (wup_hbm, wup_ref),
        (wdown_hbm, wdown_ref),
    ]
    copies = [
        pltpu.make_async_copy(source, target, copied.at[k])
        for k, (source, target) in enumerate(first + later)
    ]
    for copy in copies:
        copy.start()
    for copy in copies[: len(first)]:
        copy.wait()
    table_f32[...] = table[...].astype(F32)
    vec_ref[...] = jnp.concatenate(
        [as_row(v) for v in (mask, gain_one, bias_one, out_bias, gain_two, bias_two, down_bias)]
        + [jnp.zeros((1, 256), F32)],
        axis=0,
    )
    up_row = as_row(up)
    bias_ref[...] = jnp.concatenate(
        [as_row(query), as_row(value)]
        + [up_row[:, k * 128 : k * 128 + 128] for k in range(4)]
        + [jnp.zeros((2, 128), F32)],
        axis=0,
    )
    table_rows = table.shape[0]

    position = lax.broadcasted_iota(jnp.int32, (128, WINDOW), 0) // 2
    entry = lax.broadcasted_iota(jnp.int32, (128, WINDOW), 1)
    for t in range(mine):
        which = narrow * mine + t
        begin, shift = window_of(starts[which], table_rows)
        window = table_f32[pl.ds(begin, WINDOW), :].astype(BF16)
        pick = (entry == position + shift).astype(F32).astype(BF16)
        shown = visible_tile(vis_ref, which)
        stream_ref[t * 128 : t * 128 + 128, :] = jnp.where(
            shown, tok[t].astype(F32), vec_ref[0:1, :]
        ) + nn(pick, window)
    stream = stream_ref[...]
    centre = stream - row_mean(stream)
    unit = centre * lax.rsqrt(row_mean(centre * centre) + EPS)
    normed_ref[...] = (unit * vec_ref[1:2, :] + vec_ref[2:3, :]).astype(BF16)
    for copy in copies[len(first) :]:
        copy.wait()


def split_high_low(v):
    high = v.astype(BF16).astype(F32)
    return high, v - high


def forward_kernel(
    mine, meta, stream_ref, normed_ref, cot_ref, vec_ref, bias_ref,
    wqkv_a, wout_a, wup_a, wdown_a, wqkv_b, wout_b, wup_b, wdown_b, biases_b,
    act_ref, hidden_ref, qkv, probs_ref, gh_ref, part_ref, wqkv_all, wout_all, own_ref, oth_ref,
    context, grad_pre_all, acc, sums,
):
    for c in range(3):
        wqkv_all[:, c * 256 : c * 256 + 128] = wqkv_a[c]
        wqkv_all[:, c * 256 + 128 : c * 256 + 256] = wqkv_b[c]
    wout_all[0:128, :] = wout_a[...]
    wout_all[128:256, :] = wout_b[...]
    sums[...] = jnp.zeros_like(sums)
    rows = mine * 128
    far_biases = as_row(biases_b)
    scaled = head_masks(1.0 / math.sqrt(HEAD_DIM))
    row = lax.broadcasted_iota(jnp.int32, (128, 128), 0)
    tall = [(row < HEAD_DIM).astype(F32).astype(BF16), (row >= HEAD_DIM).astype(F32).astype(BF16)]

    def vec(k):
        return vec_ref[k : k + 1, :]

    for c in range(3):
        part = nn(normed_ref[:, :], wqkv_all[:, c * 256 : c * 256 + 256])
        if c != 1:
            k = c // 2
            other = far_biases[:, k * 128 : k * 128 + 128]
            part = part + jnp.concatenate([bias_ref[k : k + 1, :], other], axis=1)
        qkv[:, c * 256 : c * 256 + 256] = part.astype(BF16)
    places = [
        (slice(t * 128, t * 128 + 128), slice(t * 128, t * 128 + 128), pair)
        for t in range(mine)
        for pair in range(2)
    ]
    scores = [
        nt(
            qkv[at, 256 + pair * 128 : 384 + pair * 128],
            masked_pair(qkv[at, pair * 128 : pair * 128 + 128], scaled),
        )
        for at, to, pair in places
    ]
    stacked = []
    for (at, to, pair), score in zip(places, scores):
        lifted = jnp.exp(score - jnp.max(score, axis=0, keepdims=True))
        probs = (lifted * (1.0 / jnp.sum(lifted, axis=0, keepdims=True))).astype(BF16)
        probs_ref[at, pair * 256 : pair * 256 + 256] = probs
        stacked.append(side_to_stack(probs))
    for (at, to, pair), probs in zip(places, stacked):
        values = jnp.transpose(qkv[at, 512 + pair * 128 : 640 + pair * 128])
        values = jnp.concatenate([values * tall[0], values * tall[1]], axis=1)
        context[pair * 128 : pair * 128 + 128, to] = nn(values, probs).astype(BF16)
    stream = stream_ref[:, :]
    branch = tn(context[...], wout_all[...]) + vec(3)
    hidden = stream + branch
    hidden_ref[:, :] = hidden
    centre_two = hidden - row_mean(hidden)
    scale_two = lax.rsqrt(row_mean(centre_two * centre_two) + EPS)
    unit_two = centre_two * scale_two
    normed_two = (unit_two * vec(4) + vec(5)).astype(BF16)
    cot = cot_ref[...].reshape(rows, 256)
    cot_f32 = cot.astype(F32)

    def mlp_products(c):
        up, down = (wup_a, wdown_a) if c < 2 else (wup_b, wdown_b)
        at = slice((c % 2) * 256, (c % 2) * 256 + 256)
        return nn(normed_two, up[:, at]), nt(cot, down[at, :])

    refs = (own_ref, oth_ref)
    size = FIRST_ROWS // 4

    def place(quarter, begin, count):
        first = jnp.bitwise_xor(meta[1], quarter) * size + begin
        return pl.ds(pl.multiple_of(first, 16), count)

    products = mlp_products(0)
    for c in range(4):
        following = mlp_products(c + 1) if c < 3 else None
        if c < 2:
            shift = jnp.concatenate([bias_ref[2 + 2 * c + k : 3 + 2 * c + k, :] for k in range(2)], axis=1)
        else:
            shift = far_biases[:, 256 + (c % 2) * 256 : 512 + (c % 2) * 256]
        act, grad_pre, folded = by_blocks(
            functools.partial(gelu_and_slope, shift), 16, *products
        )
        sums[9 + c] += fold_rows(folded)
        act_ref[:, c * 256 : c * 256 + 256] = act
        grad_pre_all[:, c * 256 : c * 256 + 256] = grad_pre
        products = following
    grad_normed = nt(grad_pre_all[:, :512], wup_a[...]) + nt(grad_pre_all[:, 512:], wup_b[...])
    incoming = grad_normed * vec(4)
    grad_hidden = cot_f32 + scale_two * (
        incoming - row_mean(incoming) - unit_two * row_mean(incoming * unit_two)
    )
    grad_attn = grad_hidden.astype(BF16)
    sums[4] += fold_rows(grad_normed * unit_two)
    sums[5] += fold_rows(grad_normed)
    gh_ref[:, :] = grad_hidden
    out_w = nn(context[...], grad_attn)
    acc[...] = out_w
    for which, piece in enumerate((tn(grad_pre_all[...], normed_two), tn(act_ref[...], cot))):
        for side in range(2):
            for quarter in range(4):
                base = side * 512 + quarter * 128
                block = piece[base : base + 128, :].astype(BF16)
                for half in range(2):
                    at = place(quarter, which * 256 + half * 128, 128)
                    refs[side][at, :] = block[:, half * 128 : half * 128 + 128]
    for side in range(2):
        for quarter in range(4):
            rows_at = side * 128 + (quarter % 2) * 64
            lanes_at = (quarter // 2) * 128
            piece = acc[rows_at : rows_at + 64, lanes_at : lanes_at + 128]
            refs[side][place(quarter, 512, 64), :] = piece.astype(BF16)
    for k in (4, 5, 9, 10, 11, 12):
        part_ref[k : k + 1, :] = jnp.sum(sums[k], axis=0, keepdims=True)


def output_kernel(
    act_ref, hidden_ref, stream_ref, cot_ref, vec_ref, wdown_a, wdown_b, out_ref, sums_ref
):
    sums = [jnp.zeros((8, 256), F32) for _ in range(4)]
    for k in range(0, out_ref.shape[0], 2):
        at = slice(k * 128, k * 128 + 256)
        mlp = nn(act_ref[at, :512], wdown_a[...]) + nn(act_ref[at, 512:], wdown_b[...]) + vec_ref[6:7, :]
        hidden = hidden_ref[at, :]
        out_ref[k : k + 2] = (hidden + mlp).astype(BF16).reshape(2, 128, 256)
        stream = stream_ref[at, :]
        branch = hidden - stream
        sums[0] = sums[0] + fold_rows(stream * stream)
        sums[1] = sums[1] + fold_rows(branch * branch)
        sums[2] = sums[2] + fold_rows(mlp * mlp)
        sums[3] = sums[3] + fold_rows(cot_ref[k : k + 2].reshape(256, 256).astype(F32))
    for k in range(4):
        sums_ref[k] = sums[k]


def backward_kernel(
    mine, meta, starts_hbm, vis_ref, vec_ref, wqkv_all, wout_all,
    stream_ref, normed_ref, qkv, probs_ref, gh_ref, part_ref, sums_ref,
    in_grad_ref, own_ref, oth_ref,
    starts, grad_all, acc, sums, copied,
):
    narrow = meta[0]
    copy = pltpu.make_async_copy(starts_hbm, starts, copied)
    copy.start()
    acc[:, TIME_AT:, :] = jnp.zeros((2, SECOND_ROWS - TIME_AT, 128), F32)
    sums[...] = jnp.zeros_like(sums)
    rows = mine * 128
    scaled = head_masks(1.0 / math.sqrt(HEAD_DIM))
    plain = head_masks(1.0)
    copy.wait()

    grad_attn = gh_ref[:, :].astype(BF16)
    sums[3] += fold_rows(grad_attn.astype(F32))
    grad_ctx = nt(grad_attn, wout_all[...]).astype(BF16)
    places = [
        (slice(t * 128, t * 128 + 128), pair)
        for t in range(mine)
        for pair in range(2)
    ]
    pieces = [
        masked_pair(grad_ctx[t * 128 : t * 128 + 128, pair * 128 : pair * 128 + 128], plain)
        for t in range(mine)
        for pair in range(2)
    ]
    grad_probs = [
        nt(qkv[at, 512 + pair * 128 : 640 + pair * 128], piece)
        for (at, pair), piece in zip(places, pieces)
    ]
    for (at, pair), piece in zip(places, pieces):
        probs = probs_ref[at, pair * 256 : pair * 256 + 256]
        grad_all[at, 512 + pair * 128 : 640 + pair * 128] = nn(probs, piece).astype(BF16)
    grad_scores = []
    for (at, pair), grad in zip(places, grad_probs):
        weight = probs_ref[at, pair * 256 : pair * 256 + 256].astype(F32)
        inner = jnp.sum(grad * weight, axis=0, keepdims=True)
        grad_scores.append((weight * (grad - inner)).astype(BF16))
    for (at, pair), grad in zip(places, grad_scores):
        queries = masked_pair(qkv[at, pair * 128 : pair * 128 + 128], scaled)
        keys = masked_pair(qkv[at, 256 + pair * 128 : 384 + pair * 128], scaled)
        grad_all[at, pair * 128 : pair * 128 + 128] = tn(side_to_stack(grad), keys).astype(BF16)
        grad_all[at, 256 + pair * 128 : 384 + pair * 128] = nn(grad, queries).astype(BF16)
    sums[7] += fold_rows(grad_all[:, 0:256].astype(F32))
    sums[8] += fold_rows(grad_all[:, 512:768].astype(F32))
    stream = stream_ref[:, :]
    centre = stream - row_mean(stream)
    scale = lax.rsqrt(row_mean(centre * centre) + EPS)
    unit = centre * scale
    grad_normed = nt(grad_all[:, :], wqkv_all[...])
    sums[1] += fold_rows(grad_normed * unit)
    sums[2] += fold_rows(grad_normed)
    incoming = grad_normed * vec_ref[1:2, :]
    grad_stream = gh_ref[:, :] + scale * (
        incoming - row_mean(incoming) - unit * row_mean(incoming * unit)
    )
    for t in range(mine):
        which = narrow * mine + t
        piece = grad_stream[t * 128 : t * 128 + 128, :]
        shown = visible_tile(vis_ref, which)
        in_grad_ref[t] = jnp.where(shown, piece, 0.0).astype(BF16)
        sums[0] += fold_rows(jnp.where(shown, 0.0, piece))
        begin, shift = window_of(starts[which], 1000)
        position = lax.broadcasted_iota(jnp.int32, (WINDOW, 128), 1)
        entry = lax.broadcasted_iota(jnp.int32, (WINDOW, 128), 0)
        pick = (entry == position // 2 + shift).astype(F32).astype(BF16)
        high = piece.astype(BF16)
        low = (piece - high.astype(F32)).astype(BF16)
        added = nn(jnp.concatenate([pick, pick], axis=1), jnp.concatenate([high, low], axis=0))
        for lane_half in range(2):
            side = jnp.bitwise_xor(lane_half, narrow)
            acc[side, pl.ds(TIME_AT + begin, WINDOW), :] += added[
                :, lane_half * 128 : lane_half * 128 + 128
            ]
    normed_t = jnp.transpose(normed_ref[...])
    for c in range(3):
        grad_w = nn(normed_t, grad_all[:, c * 256 : c * 256 + 256])
        for side in range(2):
            acc[side, c * 256 : c * 256 + 256, :] = grad_w[:, side * 128 : side * 128 + 128]
    full = [jnp.sum(sums[k], axis=0, keepdims=True) for k in range(9)]
    for k in (4, 5):
        full[k] = part_ref[k : k + 1, :]
    full[6] = jnp.sum(sums_ref[3], axis=0, keepdims=True)
    shared = jnp.concatenate(full[:7] + [jnp.zeros((1, 256), F32)], axis=0)
    for lane_half in range(2):
        side = jnp.bitwise_xor(lane_half, narrow)
        acc[side, SMALL_AT : SMALL_AT + 8, :] = shared[:, lane_half * 128 : lane_half * 128 + 128]
    lane = lax.broadcasted_iota(jnp.int32, (1, 128), 1)
    squares = jnp.zeros((1, 128), F32)
    for k in range(3):
        row = jnp.sum(sums_ref[k], axis=0, keepdims=True)
        squares = jnp.where(lane == k, jnp.sum(row, axis=-1, keepdims=True), squares)
    for side in range(2):
        lanes = slice(side * 128, side * 128 + 128)
        small = [full[7][:, lanes], full[8][:, lanes]]
        for k in range(2):
            up_sum = part_ref[9 + side * 2 + k : 10 + side * 2 + k, :]
            small += [up_sum[:, :128], up_sum[:, 128:]]
        small += split_high_low(squares)
        acc[side, SMALL_AT + 8 : SMALL_AT + 16, :] = jnp.concatenate(small, axis=0)
    pack(meta[1], acc, own_ref, oth_ref)


def unpack_early_kernel(meta, *refs):
    parts, (up_ref, down_ref, out_w_ref) = refs[0:4], refs[4:]
    for j in range(4):
        quarter = jnp.bitwise_xor(meta[1], j)
        lanes = pl.ds(pl.multiple_of(quarter * 128, 128), 128)
        for half in range(2):
            at = slice(half * 128, half * 128 + 128)
            up_ref[at, lanes] = jnp.transpose(parts[j][at, :].astype(F32))
            down_ref[lanes, at] = parts[j][256 + half * 128 : 384 + half * 128, :].astype(F32)
        rows = pl.ds(pl.multiple_of((quarter % 2) * 64, 64), 64)
        lanes = pl.ds(pl.multiple_of((quarter // 2) * 128, 128), 128)
        out_w_ref[rows, lanes] = parts[j][512:576, :].astype(F32)


def unpack_late_kernel(scale, meta, *refs):
    parts, peer_parts = refs[0:4], refs[4:8]
    qkv_hbm, time_hbm, *row_hbms = refs[8:21]
    late, *rows, copied = refs[21:]
    narrow, place = meta[0], meta[1]
    for j in range(4):
        at = rows_of(jnp.bitwise_xor(place, j), SECOND_ROWS // 4)
        late[0, at, :] = parts[j][...].astype(F32)
        late[1, at, :] = peer_parts[j][...].astype(F32)
    time_rows = time_hbm.shape[0]
    moves = [(late.at[0, pl.ds(c * 256, 256)], qkv_hbm.at[c]) for c in range(3)]
    for lane_half in range(2):
        side = jnp.bitwise_xor(lane_half, narrow)
        source = late.at[side, pl.ds(TIME_AT, time_rows)]
        moves.append((source, time_hbm.at[:, pl.ds(lane_half * 128, 128)]))
    small = late[0, SMALL_AT + 8 : SMALL_AT + 16, :]
    shared = [late[jnp.bitwise_xor(half, narrow), SMALL_AT : SMALL_AT + 8, :] for half in range(2)]
    shared = jnp.concatenate(shared, axis=1)
    copies = [pltpu.make_async_copy(*move, copied.at[k]) for k, move in enumerate(moves)]
    for copy in copies:
        copy.start()
    for k in range(7):
        rows[k][...] = shared[k : k + 1, :]
    rows[7][...] = small[0:1, :]
    rows[8][...] = small[1:2, :]
    for k in range(4):
        rows[9][:, k * 128 : k * 128 + 128] = small[2 + k : 3 + k, :]
    row_copies = [
        pltpu.make_async_copy(row, target, copied.at[len(moves) + k])
        for k, (row, target) in enumerate(zip(rows, row_hbms))
    ]
    rows[10][...] = jnp.sqrt((small[6:7, :3] + small[7:8, :3]) * scale)
    for copy in row_copies:
        copy.start()
    for copy in copies + row_copies:
        copy.wait()


def swap_narrow(v):
    return lax.ppermute(v, "narrow", [(0, 1), (1, 0)])


def exchange(v, flip):
    count = lax.axis_size("wide")
    return lax.ppermute(v, "wide", [(d, d ^ flip) for d in range(count)])


def plane_send(own, received, order=(1, 2, 3)):
    size = own.shape[0] // 4
    sums = [pair_sum(own[k * size : k * size + size], received[k * size : k * size + size]) for k in (1, 2, 3)]
    sent = {k: exchange(sums[k - 1], k) for k in order}
    return [sent[k] for k in (1, 2, 3)]


def plane_sum(own, received, arrived):
    size = own.shape[0] // 4
    total = own[:size].astype(F32) + received[:size].astype(F32)
    for piece in arrived:
        total = total + piece.astype(F32)
    return total.astype(BF16)


def pair_sum(kept, arrived):
    return (kept.astype(F32) + arrived.astype(F32)).astype(BF16)


def plane_gather(block):
    return [block] + [exchange(block, j) for j in (1, 2, 3)]


def tied(first, second):
    return lax.optimization_barrier((first, second))


def whole(shape):
    return pl.BlockSpec(shape, lambda *_: (0,) * len(shape))


def per_device(
    tokens_in, visible, traj_start, cotangent, mask_token, time_table, gain_one, bias_one,
    w_qkv, query_bias, value_bias, w_out, out_bias, gain_two, bias_two, w_up, up_bias,
    w_down, down_bias,
):
    traj_count, seq_len, width = tokens_in.shape
    wide_count = lax.axis_size("wide")
    assert wide_count % 8 == 0
    mine = traj_count // lax.axis_size("narrow")
    token_rows = mine * seq_len
    narrow = lax.axis_index("narrow")
    meta = jnp.stack([narrow, jnp.bitwise_and(lax.axis_index("wide"), 3)]).astype(jnp.int32)
    w_qkv = jnp.transpose(w_qkv, (1, 0, 2))
    biases = jnp.concatenate([query_bias, value_bias, up_bias])
    swapped = [swap_narrow(v) for v in (w_qkv, w_out, w_up, w_down, biases)]
    scalars = pl.BlockSpec(memory_space=pltpu.SMEM)
    vmem = pl.BlockSpec(memory_space=pltpu.VMEM)
    hbm = pl.BlockSpec(memory_space=pltpu.HBM)
    params = pltpu.CompilerParams(vmem_limit_bytes=VMEM_LIMIT)

    def shaped(shape, dtype):
        return jax.ShapeDtypeStruct(shape, dtype)

    half = shaped((mine, seq_len, width), BF16)
    tokens_f32 = shaped((token_rows, 256), F32)
    tokens_bf16 = shaped((token_rows, 256), BF16)
    inputs = (
        traj_start, tokens_in, visible, cotangent, time_table, mask_token, gain_one, bias_one,
        out_bias, gain_two, bias_two, down_bias, w_qkv, w_out, w_up, w_down, query_bias, value_bias,
        up_bias,
    )
    inputs = [pltpu.with_memory_space_constraint(v, pltpu.HBM) for v in inputs]
    vectors = [mask_token, gain_one, bias_one, out_bias, gain_two, bias_two, down_bias]
    vectors += [query_bias, value_bias, up_bias]
    stream, normed, cot, vecs, biases, shown, *weights = pl.pallas_call(
        functools.partial(embed_kernel, mine),
        in_specs=[scalars] + [hbm] * len(inputs),
        out_specs=[vmem] * 10,
        out_shape=[
            tokens_f32, tokens_bf16, half, shaped((8, 256), F32), shaped((8, 128), F32),
            shaped(visible.shape, jnp.int32),
            *[shaped(v.shape, BF16) for v in (w_qkv, w_out, w_up, w_down)],
        ],
        scratch_shapes=[
            pltpu.SMEM(traj_start.shape, jnp.int32),
            pltpu.VMEM(half.shape, BF16),
            pltpu.VMEM(time_table.shape, BF16),
            pltpu.VMEM(time_table.shape, F32),
            *[pltpu.VMEM(v.shape, v.dtype) for v in vectors],
            pltpu.SemaphoreType.DMA((len(inputs),)),
        ],
        compiler_params=params,
        cost_estimate=pl.CostEstimate(
            flops=2 * token_rows * 128 * 256, bytes_accessed=6000000, transcendentals=token_rows
        ),
        name="embed_and_first_norm",
    )(meta, *inputs)

    first = shaped((FIRST_ROWS, 128), BF16)
    second = shaped((SECOND_ROWS, 128), BF16)
    hidden_units = shaped((token_rows, 1024), BF16)
    act, hidden, qkv, probs, grad_hidden, part, wqkv_all, wout_all, own, oth = pl.pallas_call(
        functools.partial(forward_kernel, mine),
        in_specs=[scalars] + [vmem] * 14,
        out_specs=[vmem] * 10,
        out_shape=[
            hidden_units, tokens_f32, shaped((token_rows, 768), BF16), shaped((token_rows, 512), BF16),
            tokens_f32, shaped((16, 256), F32), shaped((256, 768), BF16), shaped((256, 256), BF16), first,
            first,
        ],
        scratch_shapes=[
            pltpu.VMEM((256, mine * 128), BF16),
            pltpu.VMEM(hidden_units.shape, BF16),
            pltpu.VMEM((256, 256), F32),
            pltpu.VMEM((16, 8, 256), F32),
        ],
        compiler_params=params,
        cost_estimate=pl.CostEstimate(
            flops=2 * token_rows * 1900000, bytes_accessed=12000000, transcendentals=token_rows * 1600
        ),
        name="forward_and_mlp_backward",
    )(meta, stream, normed, cot, vecs, biases, *weights, *swapped)

    received = swap_narrow(oth)
    arrived = plane_send(own, received)
    out_half, squares = pl.pallas_call(
        output_kernel,
        in_specs=[vmem] * 7,
        out_specs=[vmem] * 2,
        out_shape=[half, shaped((4, 8, 256), F32)],
        compiler_params=params,
        cost_estimate=pl.CostEstimate(
            flops=2 * token_rows * 270000, bytes_accessed=4000000, transcendentals=0
        ),
        name="mlp_output",
    )(act, hidden, stream, cot, vecs, weights[3], swapped[3])
    in_half, second_own, second_oth = pl.pallas_call(
        functools.partial(backward_kernel, mine),
        in_specs=[scalars, hbm] + [vmem] * 11,
        out_specs=[vmem] * 3,
        out_shape=[half, second, second],
        scratch_shapes=[
            pltpu.SMEM(traj_start.shape, jnp.int32),
            pltpu.VMEM((token_rows, 768), BF16),
            pltpu.VMEM((2, SECOND_ROWS, 128), F32),
            pltpu.VMEM((9, 8, 256), F32),
            pltpu.SemaphoreType.DMA,
        ],
        compiler_params=params,
        cost_estimate=pl.CostEstimate(
            flops=2 * token_rows * 1000000, bytes_accessed=8000000, transcendentals=0
        ),
        name="attention_backward",
    )(
        meta, inputs[0], shown, vecs, wqkv_all, wout_all, stream, normed, qkv, probs, grad_hidden, part,
        squares,
    )

    flips = [1 << k for k in range(2, wide_count.bit_length() - 1)]
    out_received = swap_narrow(out_half)
    second_oth, arrived, out_received = lax.optimization_barrier((second_oth, arrived, out_received))
    block = plane_sum(own, received, arrived)
    second_received = swap_narrow(second_oth)
    moved = exchange(block, flips[-1])
    second_arrived = plane_send(second_own, second_received, (2, 1, 3))
    moved, second_arrived[2] = tied(moved, second_arrived[2])
    block = pair_sum(block, moved)
    for flip in flips[-2::-1]:
        block = pair_sum(block, exchange(block, flip))
    second_block = plane_sum(second_own, second_received, second_arrived)
    in_half, second_block = tied(in_half, second_block)
    in_received = swap_narrow(in_half)
    moved = exchange(second_block, flips[0])
    moved, in_received = tied(moved, in_received)
    second_block = pair_sum(second_block, moved)
    first_parts = plane_gather(block)
    for flip in flips[1:]:
        second_block = pair_sum(second_block, exchange(second_block, flip))
    block = second_block

    row = shaped((1, 256), F32)
    half_row = shaped((1, 128), F32)
    shapes = [shaped((256, 512), F32), shaped((512, 256), F32), shaped((128, 256), F32)]
    grad_up, grad_down, grad_out_w = pl.pallas_call(
        unpack_early_kernel,
        grid_spec=pltpu.PrefetchScalarGridSpec(
            num_scalar_prefetch=1,
            grid=(1,),
            in_specs=[whole(v.shape) for v in first_parts],
            out_specs=[whole(v.shape) for v in shapes],
        ),
        out_shape=shapes,
        compiler_params=params,
        cost_estimate=pl.CostEstimate(flops=0, bytes_accessed=10000000, transcendentals=0),
        name="unpack_early",
    )(meta, *first_parts)
    second_parts = plane_gather(block)
    def both_halves(kept, received):
        return jnp.where(
            narrow == 0,
            jnp.concatenate(kept + received, axis=0),
            jnp.concatenate(received + kept, axis=0),
        )

    output = both_halves([out_half], [out_received])
    input_grad = both_halves([in_half], [in_received])
    second_parts[3], grad_out_w = tied(second_parts[3], grad_out_w)
    peer_parts = [swap_narrow(v) for v in second_parts]
    row_shapes = [row] * 7 + [half_row] * 2 + [shaped((1, 512), F32), shaped((1, 3), F32)]
    out_shape = [shaped((3, 256, 128), F32), shaped(time_table.shape, F32)] + row_shapes
    (
        grad_qkv, grad_time, grad_mask_token, grad_gain_one, grad_bias_one, grad_out_bias,
        grad_gain_two, grad_bias_two, grad_down_bias, grad_query_bias, grad_value_bias, grad_up_bias,
        stats,
    ) = pl.pallas_call(
        functools.partial(unpack_late_kernel, 1.0 / (traj_count * wide_count * seq_len * width)),
        in_specs=[scalars] + [vmem] * 8,
        out_specs=[hbm] * 13,
        out_shape=out_shape,
        scratch_shapes=[
            pltpu.VMEM((2, SECOND_ROWS, 128), F32),
            *[pltpu.VMEM(v.shape, F32) for v in row_shapes],
            pltpu.SemaphoreType.DMA((16,)),
        ],
        compiler_params=params,
        cost_estimate=pl.CostEstimate(flops=0, bytes_accessed=10000000, transcendentals=0),
        name="unpack_late",
    )(meta, *second_parts, *peer_parts)
    return (
        output, input_grad, grad_mask_token[0], grad_time, grad_gain_one[0], grad_bias_one[0],
        jnp.transpose(grad_qkv, (1, 0, 2)), grad_query_bias[0], grad_value_bias[0], grad_out_w,
        grad_out_bias[0], grad_gain_two[0], grad_bias_two[0], grad_up, grad_up_bias[0], grad_down,
        grad_down_bias[0], stats[0],
    )


def solution(mesh):
    placed = (
        P("wide", None, None), P("wide", None), P("wide"), P("wide", None, None), P(), P(), P(), P(),
        P(None, None, "narrow"), P("narrow"), P("narrow"), P("narrow", None), P(), P(), P(),
        P(None, "narrow"), P("narrow"), P("narrow", None), P(),
    )
    return jax.shard_map(
        per_device,
        mesh=mesh,
        in_specs=placed,
        out_specs=(
            P("wide", None, None), P("wide", None, None), P(), P(), P(), P(),
            P(None, None, "narrow"), P("narrow"), P("narrow"), P("narrow", None), P(), P(), P(),
            P(None, "narrow"), P("narrow"), P("narrow", None), P(), P(),
        ),
        check_vma=False,
    )
```
